256 devices in a mesh: tok: 16 (over z_lo, y, core), feat: 16 (over x, z_hi).
Axes of the slice: x: 4, y: 4, z: 8 (z_hi: 4, z_lo: 2; z = z_hi * 2 + z_lo), core: 2. Of those that a mesh axis runs over, the one named last changes fastest.
Arguments:
- tokens: bfloat16 [16384, 2048], P('tok', 'feat'), may hold values from -6 to 6
- level_bits: int32 [2, 4], replicated, may hold values from 0 to 3, each once within a row
- up_blocks: bfloat16 [2, 16, 5, 128, 512], P(None, 'feat', None, None, 'tok'), may hold values from -0.21875 to 0.21875
- down_blocks: bfloat16 [2, 16, 5, 512, 128], P(None, 'feat', None, None, 'tok'), may hold values from -0.109375 to 0.109375
- rank_in: bfloat16 [2, 2048, 256], replicated, may hold values from -0.125 to 0.125
- rank_up: bfloat16 [2, 256, 8192], P(None, None, 'feat'), may hold values from -0.15625 to 0.15625
- rank_down: bfloat16 [2, 8192, 256], P(None, 'feat'), may hold values from -0.0625 to 0.0625
- rank_out: bfloat16 [2, 256, 2048], P(None, None, 'feat'), may hold values from -0.15625 to 0.15625
Outputs:
- outputs: bfloat16 [16384, 2048], P('tok', 'feat')
The draws below stay inside these ranges and needn't reach their ends.
Inputs may be any that keep to these rules, and one draw needn't show every extreme that they name: `level_bits`: each row is a permutation of the bits 0 to 3.
All inputs are finite; a program needn't handle non-finite values.
Results may differ from the reference program's by a relative error of at most 0.015.
Values may be sent and summed in bfloat16 or wider, within the bound.
No kernel may reach another device: no remote copies, remote signals or barrier semaphores. Data moves between devices by JAX's collectives and lax.ppermute only.
A program may use at most 64 MiB of HBM per device.

```python
import jax
import jax.numpy as jnp
from jax import lax

D = 2048
HID = 8192
NB = 16
LEVELS = 4
RANK = 256
LAYERS = 2
TOK_DEV = 1024
TOKENS = 16384


def levels(rng, shape, cuts, smallest, largest):
    level = 1.0
    for dim, shards_of in cuts:
        heights = jax.random.uniform(jax.random.fold_in(jax.random.fold_in(rng, 6), dim), (shards_of,), jnp.float32, smallest / len(cuts), largest / len(cuts))
        level = level * jnp.repeat(jnp.exp(heights), shape[dim] // shards_of).reshape((-1,) + (1,) * (len(shape) - 1 - dim))
    return level


def centred(key, dims, scale, most, pieces=(), kind=jnp.bfloat16):
    drawn = jax.random.normal(key, dims, jnp.float32) * scale
    if len(pieces) > 0:
        drawn = levels(key, dims, pieces, -0.22, 0.18) * drawn
    return jnp.clip(drawn, min=-most, max=most).astype(kind)


def setup_inputs(seed: int = 0) -> dict:
    seeds = jax.random.split(jax.random.key(seed), 9)
    tokens = centred(seeds[0], (TOKENS, D), 1.0, 6.0, ((0, 16), (1, 16)))
    level_bits = jax.vmap(lambda own: jax.random.permutation(own, LEVELS))(jax.random.split(seeds[1], LAYERS)).reshape((LAYERS, LEVELS)).astype(jnp.int32)
    up_blocks = centred(seeds[2], (LAYERS, NB, LEVELS + 1, D // NB, HID // NB), ((LEVELS + 2) * (D // NB)) ** -0.5, 0.21875, ((1, 16), (4, 16)))
    down_blocks = centred(seeds[3], (LAYERS, NB, LEVELS + 1, HID // NB, D // NB), ((LEVELS + 2) * (HID // NB)) ** -0.5, 0.109375, ((1, 16), (4, 16)))
    rank_in = centred(seeds[4], (LAYERS, D, RANK), D ** -0.5, 0.125)
    rank_up = centred(seeds[5], (LAYERS, RANK, HID), ((LEVELS + 2) * RANK) ** -0.5, 0.15625, ((2, 16),))
    rank_down = centred(seeds[6], (LAYERS, HID, RANK), HID ** -0.5, 0.0625, ((1, 16),))
    rank_out = centred(seeds[7], (LAYERS, RANK, D), ((LEVELS + 2) * RANK) ** -0.5, 0.15625, ((2, 16),))
    return {"tokens": tokens, "level_bits": level_bits, "up_blocks": up_blocks, "down_blocks": down_blocks, "rank_in": rank_in, "rank_up": rank_up, "rank_down": rank_down, "rank_out": rank_out}


def block_einsum(left, right):
    return jnp.einsum("tjd,jdh->tjh", left.astype(jnp.float32), right.astype(jnp.float32))


def reference(tokens, level_bits, up_blocks, down_blocks, rank_in, rank_up, rank_down, rank_out):
    width_block = D // NB
    hidden_block = HID // NB
    block_ids = jnp.arange(NB, dtype=jnp.int32)
    current = tokens
    for layer_num in range(LAYERS):
        up_layer = up_blocks[layer_num]
        down_layer = down_blocks[layer_num]
        partners = [jnp.bitwise_xor(block_ids, jnp.left_shift(jnp.int32(1), level_bits[layer_num, level_num]).astype(jnp.int32)).astype(jnp.int32) for level_num in range(LEVELS)]

        def tile_layer(tile_rows, up_layer=up_layer, down_layer=down_layer, partners=partners, layer_num=layer_num):
            blocked = tile_rows.reshape(-1, NB, width_block)
            pre_act = block_einsum(blocked, up_layer[:, 0])
            for level_num in range(LEVELS):
                partner = jnp.take(blocked, partners[level_num], axis=1)
                pre_act = pre_act + block_einsum(partner, up_layer[:, 1 + level_num])
            latent = jnp.dot(tile_rows, rank_in[layer_num], preferred_element_type=jnp.float32).astype(jnp.bfloat16)
            pre_act = pre_act + jnp.dot(latent, rank_up[layer_num], preferred_element_type=jnp.float32).reshape(-1, NB, hidden_block)
            hidden = jax.nn.gelu(pre_act, approximate=False).astype(jnp.bfloat16)
            result = block_einsum(hidden, down_layer[:, 0])
            for level_num in range(LEVELS):
                moved = jnp.take(hidden, partners[level_num], axis=1)
                moved_weight = jnp.take(down_layer[:, 1 + level_num], partners[level_num], axis=0)
                result = result + block_einsum(moved, moved_weight)
            latent_back = jnp.dot(hidden.reshape(-1, HID), rank_down[layer_num], preferred_element_type=jnp.float32).astype(jnp.bfloat16)
            result = result + jnp.dot(latent_back, rank_out[layer_num], preferred_element_type=jnp.float32).reshape(-1, NB, width_block)
            return (tile_rows.astype(jnp.float32) + result.reshape(-1, D)).astype(jnp.bfloat16)

        tiles = current.reshape(TOKENS // TOK_DEV, TOK_DEV, D)
        current = lax.map(tile_layer, tiles).reshape(TOKENS, D)
    return current
```

```python
import jax
import jax.numpy as jnp
from jax import lax
from jax.sharding import Mesh, PartitionSpec as P

BF = jnp.bfloat16
F32 = jnp.float32
TOK = ("zl", "y1", "y0", "core")
FEAT = ("x1", "x0", "zh1", "zh0")
SWAPPED = ("zl", "core", "zh1", "zh0")
BIT_AXES = ("zl", "core", "x0", "x1")
CUBE = ("x1", "x0", "zl")


def pair(value, axis):
    return lax.ppermute(value, axis, [(0, 1), (1, 0)])


def bits(i):
    return i >> 3 & 1, i >> 2 & 1, i >> 1 & 1, i & 1


def index(zl, core, zh1, zh0):
    return zl << 3 | core << 2 | zh1 << 1 | zh0


def swap(value, k0=0, k1=0):
    perm = []
    for dst in range(16):
        zl, core, zh1, zh0 = bits(dst)
        perm.append((index(zh0 ^ k0, zh1 ^ k1, core, zl), dst))
    return lax.ppermute(value, SWAPPED, perm)


def swap_copied(value):
    perm = []
    for dst in range(16):
        zl, core, zh1, zh0 = bits(dst)
        perm.append((index(zh0 ^ zh1 ^ core, zh1, core, zl), dst))
    return lax.ppermute(value, SWAPPED, perm)


def gather_planes(shard):
    zh0, zh1 = lax.axis_index("zh0"), lax.axis_index("zh1")
    out = jnp.zeros((2, 2) + shard.shape, shard.dtype)
    zero = jnp.int32(0)
    for k0 in range(2):
        for k1 in range(2):
            got = swap(shard, k0, k1)
            out = lax.dynamic_update_slice(
                out, got[None, None], (zh0 ^ k0, zh1 ^ k1) + (zero,) * shard.ndim
            )
    return out


def gather_y(part):
    y = lax.axis_index(("y1", "y0"))
    zero = jnp.int32(0)
    out = jnp.zeros((4,) + part.shape, part.dtype)
    out = lax.dynamic_update_slice(out, part[None], (y,) + (zero,) * part.ndim)
    for step in range(1, 4):
        got = lax.ppermute(part, ("y1", "y0"), [(i, (i + step) % 4) for i in range(4)])
        out = lax.dynamic_update_slice(
            out, got[None], ((y - step) % 4,) + (zero,) * part.ndim
        )
    return out


def all_sum(part):
    core = lax.axis_index("core")
    half = part.shape[0] // 2
    mine = lax.dynamic_slice_in_dim(part, core * half, half, 0)
    other = lax.dynamic_slice_in_dim(part, (1 - core) * half, half, 0)
    mine = (mine.astype(F32) + pair(other, "core").astype(F32)).astype(BF)
    mine = mine.reshape(8, half // 8, part.shape[1])
    terms = lax.all_to_all(mine, CUBE, 0, 0)
    total = jnp.sum(terms.astype(F32), axis=0).astype(BF)
    mine = lax.all_to_all(jnp.broadcast_to(total[None], mine.shape), CUBE, 0, 0)
    mine = mine.reshape(half, part.shape[1])
    other = pair(mine, "core")
    first = core == 0
    return jnp.concatenate(
        [jnp.where(first, mine, other), jnp.where(first, other, mine)], axis=0
    )


def per_device(tokens, level_bits, up_blocks, down_blocks, rank_in, rank_up, rank_down, rank_out):
    layers = level_bits.shape[0]
    block = (
        lax.axis_index("x1") * 8
        + lax.axis_index("x0") * 4
        + lax.axis_index("core") * 2
        + lax.axis_index("zl")
    )
    width = tokens.shape[1]
    x = swap(tokens)
    up_shard = up_blocks[:, 0].transpose(0, 1, 3, 2).reshape(layers, 160, 128)
    down_shard = (
        down_blocks[:, 0].reshape(layers, 5, 4, 128, 8).transpose(0, 1, 2, 4, 3)
    ).reshape(layers, 160, 128)
    shard = jnp.concatenate([up_shard, down_shard], axis=1)
    planes = gather_planes(shard)
    rank_up, rank_down, rank_out = (swap_copied(v) for v in (rank_up, rank_down, rank_out))
    for layer in range(layers):
        got = gather_y(planes[:, :, layer])
        got = got.transpose(1, 0, 2, 3, 4)
        up_t = got[:, :, :, :160].reshape(16, 5, 32, 128).transpose(1, 0, 2, 3).reshape(5, 512, 128)
        down_t = (
            got[:, :, :, 160:].reshape(16, 5, 4, 8, 128).transpose(1, 0, 3, 2, 4)
        ).reshape(5, 128, 512)
        row = level_bits[layer]
        places = [
            1 + jnp.sum(jnp.where(row == bit, jnp.arange(4, dtype=jnp.int32), 0))
            for bit in range(4)
        ]
        order = jnp.stack([jnp.int32(0)] + places)
        up_t = jnp.take(up_t, order, axis=0)
        down_t = jnp.take(down_t, order, axis=0).reshape(640, 512)
        up_w = jnp.concatenate([up_t[i] for i in range(5)], axis=1)

        rows_in = lax.dynamic_slice_in_dim(rank_in[layer], block * width, width, 0)
        part = jnp.dot(x, rows_in, preferred_element_type=F32).astype(BF)
        latent = all_sum(part)
        partners = [pair(x, axis) for axis in BIT_AXES]
        pre = lax.dot_general(
            jnp.concatenate([x] + partners, axis=1), up_w, (((1,), (1,)), ((), ())),
            preferred_element_type=F32,
        ) + jnp.dot(latent, rank_up[layer], preferred_element_type=F32)
        hidden = jax.nn.gelu(pre, approximate=False).astype(BF)
        back = all_sum(
            jnp.dot(hidden, rank_down[layer], preferred_element_type=F32).astype(BF)
        )
        terms = lax.dot_general(
            hidden, down_t, (((1,), (1,)), ((), ())), preferred_element_type=F32
        )
        result = terms[:, :width] + jnp.dot(back, rank_out[layer], preferred_element_type=F32)
        for bit, axis in enumerate(BIT_AXES):
            term = terms[:, (1 + bit) * width : (2 + bit) * width].astype(BF)
            result = result + pair(term, axis).astype(F32)
        x = (x.astype(F32) + result).astype(BF)
    return swap(x)


def solution(mesh):
    fine = Mesh(mesh.devices.reshape((2,) * 8), TOK + FEAT)
    return jax.shard_map(
        per_device,
        mesh=fine,
        in_specs=(
            P(TOK, FEAT),
            P(),
            P(None, FEAT, None, None, TOK),
            P(None, FEAT, None, None, TOK),
            P(),
            P(None, None, FEAT),
            P(None, FEAT, None),
            P(None, None, FEAT),
        ),
        out_specs=P(TOK, FEAT),
        check_vma=False,
    )
```

```python
import jax
import jax.numpy as jnp
from jax import lax
from jax.experimental import pallas as pl
from jax.experimental.pallas import tpu as pltpu
from jax.sharding import Mesh, PartitionSpec as P

BF = jnp.bfloat16
F32 = jnp.float32
TOK = ("zl", "y1", "y0", "core")
FEAT = ("x1", "x0", "zh1", "zh0")
SWAPPED = ("zl", "core", "zh1", "zh0")
BIT_AXES = ("zl", "core", "x0", "x1")
CUBE = ("x1", "x0", "zl")


def pair(value, axis):
    return lax.ppermute(value, axis, [(0, 1), (1, 0)])


def bits(i):
    return i >> 3 & 1, i >> 2 & 1, i >> 1 & 1, i & 1


def index(zl, core, zh1, zh0):
    return zl << 3 | core << 2 | zh1 << 1 | zh0


def swap(value, k0=0, k1=0):
    perm = []
    for dst in range(16):
        zl, core, zh1, zh0 = bits(dst)
        perm.append((index(zh0 ^ k0, zh1 ^ k1, core, zl), dst))
    return lax.ppermute(value, SWAPPED, perm)


def swap_copied(value):
    perm = []
    for dst in range(16):
        zl, core, zh1, zh0 = bits(dst)
        perm.append((index(zh0 ^ zh1 ^ core, zh1, core, zl), dst))
    return lax.ppermute(value, SWAPPED, perm)


def copied_all_to_all(value, count, axes):
    return lax.all_to_all(jnp.broadcast_to(value[None], (count,) + value.shape), axes, 0, 0)


def after(value, *others):
    return lax.optimization_barrier((value,) + others)[0]


def nt_dot(left, right):
    return lax.dot_general(left, right, (((1,), (1,)), ((), ())), preferred_element_type=F32)


def dot(left, right):
    return jnp.dot(left, right, preferred_element_type=F32)


TILE = 256
TILES = 4
TOKENS = TILE * TILES
HALF = TOKENS // 2
WIDTH = 128
HIDDEN = 512
RANK = 256
LIMIT = pltpu.CompilerParams(vmem_limit_bytes=56 << 20)


def ordered(rows):
    core = lax.axis_index("core")
    half = rows.shape[0] // 2
    return jnp.where(core == 0, rows, jnp.concatenate([rows[half:], rows[:half]], axis=0))


def prep_kernel(order, cols, up_w, down_w):
    for place in range(5):
        at = pl.multiple_of(order[place] * 32, 32)
        for zl in range(2):
            for y in range(4):
                for core in range(2):
                    t = zl * 8 + y * 2 + core
                    up_w[t * 32 : (t + 1) * 32, place * WIDTH : (place + 1) * WIDTH] = cols[
                        y, zl * 2 + core, pl.ds(at, 32), :
                    ]
                pieces = [
                    cols[y, zl * 2 + core, pl.ds(160 + at, 32), :].astype(F32) for core in range(2)
                ]
                top = place * WIDTH + zl * 64 + y * 16
                for q in range(4):
                    down_w[top : top + 16, q * 128 : (q + 1) * 128] = jnp.concatenate(
                        [piece[q * 8 : (q + 1) * 8] for piece in pieces], axis=0
                    ).astype(BF)


def prep(order, cols):
    shapes = [(HIDDEN, 5 * WIDTH), (5 * WIDTH, HIDDEN)]
    return pl.pallas_call(
        prep_kernel,
        grid_spec=pltpu.PrefetchScalarGridSpec(
            num_scalar_prefetch=1,
            grid=(1,),
            in_specs=[pl.BlockSpec((4, 4, 320, 128), lambda i, order: (0, 0, 0, 0))],
            out_specs=[pl.BlockSpec(shape, lambda i, order: (0, 0)) for shape in shapes],
        ),
        out_shape=[jax.ShapeDtypeStruct(shape, BF) for shape in shapes],
        compiler_params=LIMIT,
        cost_estimate=pl.CostEstimate(flops=1 << 20, bytes_accessed=3 << 20, transcendentals=0),
        name="prep",
    )(order, cols)


def gelu(value):
    return 0.5 * value * (1.0 + lax.erf(value * (0.5**0.5)))


def mlp_kernel(
    x, p_zl, p_core, p_x0, p_x1, mine, other, up_w, down_w, rank_up, rank_down,
    mine_back, other_back, own, t_zl, t_core, t_x0, t_x1,
):
    i = pl.program_id(0)
    value = x[...]
    left = jnp.concatenate([value, p_zl[...], p_core[...], p_x0[...], p_x1[...]], axis=1)
    latent = jnp.where(i < 2, mine[...], other[...])
    pre = nt_dot(left, up_w[...]) + dot(latent, rank_up[...])
    hidden = gelu(pre).astype(BF)
    share = dot(hidden, rank_down[...]).astype(BF)

    @pl.when(i < 2)
    def _():
        mine_back[...] = share

    @pl.when(i >= 2)
    def _():
        other_back[...] = share

    terms = nt_dot(hidden, down_w[...])
    own[...] = value.astype(F32) + terms[:, :WIDTH]
    for bit, out in enumerate((t_zl, t_core, t_x0, t_x1)):
        out[...] = terms[:, (1 + bit) * WIDTH : (2 + bit) * WIDTH].astype(BF)


def mlp(x, partners, latent, weights, rank_up, rank_down):
    row = pl.BlockSpec((TILE, WIDTH), lambda i: (i, 0))
    partner_row = pl.BlockSpec((TILE, WIDTH), lambda i: ((i + 2) % TILES, 0))
    halves = [
        pl.BlockSpec((TILE, RANK), lambda i: (jnp.minimum(i, 1), 0)),
        pl.BlockSpec((TILE, RANK), lambda i: (jnp.maximum(i - 2, 0), 0)),
    ]
    whole = lambda *shape: pl.BlockSpec(shape, lambda i: (0,) * len(shape))
    shape = jax.ShapeDtypeStruct
    return pl.pallas_call(
        mlp_kernel,
        grid=(TILES,),
        in_specs=[row, row, partner_row, row, row]
        + halves
        + [
            whole(HIDDEN, 5 * WIDTH),
            whole(5 * WIDTH, HIDDEN),
            whole(RANK, HIDDEN),
            whole(HIDDEN, RANK),
        ],
        out_specs=halves + [row] * 5,
        out_shape=[shape((HALF, RANK), BF)] * 2
        + [shape((TOKENS, WIDTH), F32)]
        + [shape((TOKENS, WIDTH), BF)] * 4,
        compiler_params=LIMIT,
        cost_estimate=pl.CostEstimate(
            flops=4 * TOKENS * HIDDEN * (5 * WIDTH + RANK),
            bytes_accessed=6 << 20,
            transcendentals=0,
        ),
        name="mlp",
    )(x, *partners, *latent, *weights, rank_up, rank_down)


def chip_sums(parts):
    return jnp.sum(lax.all_to_all(parts, CUBE, 0, 0).astype(F32), axis=0)


def core_sum(mine, other):
    return mine.astype(F32) + pair(other.astype(BF), "core").astype(F32)


def share_of_core(rows):
    core = lax.axis_index("core")
    half = rows.shape[0] // 2
    return (
        lax.dynamic_slice_in_dim(rows, core * half, half, 0),
        lax.dynamic_slice_in_dim(rows, (1 - core) * half, half, 0),
    )


def block_shards(up_blocks, down_blocks):
    layers = up_blocks.shape[0]
    up_shard = up_blocks[:, 0].transpose(0, 1, 3, 2).reshape(layers, 160, 128)
    down_shard = down_blocks[:, 0].reshape(layers, 5, 4, 128, 8).transpose(0, 1, 2, 4, 3)
    return jnp.concatenate([up_shard, down_shard.reshape(layers, 160, 128)], axis=1)


def gather_planes(shards):
    zh0, zh1 = lax.axis_index("zh0"), lax.axis_index("zh1")
    out = jnp.zeros(shards.shape[:1] + (2, 2) + shards.shape[1:], shards.dtype)
    for k0 in range(2):
        for k1 in range(2):
            got = swap(shards, k0, k1)
            out = lax.dynamic_update_slice(out, got[:, None, None], (0, zh0 ^ k0, zh1 ^ k1, 0, 0))
    return out


def gather_columns(plane):
    y = lax.axis_index(("y1", "y0"))
    plane = plane.reshape((1, 4) + plane.shape[2:])
    out = jnp.zeros((4,) + plane.shape[1:], plane.dtype)
    out = lax.dynamic_update_slice(out, plane, (y, 0, 0, 0))
    for step in range(1, 4):
        got = lax.ppermute(plane, ("y1", "y0"), [(i, (i + step) % 4) for i in range(4)])
        out = lax.dynamic_update_slice(out, got, ((y - step) % 4, 0, 0, 0))
    return out


def low_rank_part(x, rows_in):
    other = dot(x[HALF:], rows_in)
    return core_sum(dot(x[:HALF], rows_in), other).astype(BF).reshape(8, HALF // 8, RANK)


def exchange(blocks):
    return [pair(value, axis) for value, axis in zip(blocks, BIT_AXES)]


def per_device(tokens, level_bits, up_blocks, down_blocks, rank_in, rank_up, rank_down, rank_out):
    layers = level_bits.shape[0]
    core = lax.axis_index("core")
    block = lax.axis_index("x1") * 8 + lax.axis_index("x0") * 4 + core * 2 + lax.axis_index("zl")
    levels = jnp.arange(4, dtype=jnp.int32)
    orders = [
        jnp.stack(
            [jnp.int32(0)]
            + [1 + jnp.sum(jnp.where(level_bits[layer] == bit, levels, 0)) for bit in range(4)]
        )
        for layer in range(layers)
    ]
    rows_in = lax.dynamic_slice(rank_in, (0, block * WIDTH, 0), (layers, WIDTH, RANK))
    x = swap(tokens)
    planes = gather_planes(block_shards(up_blocks, down_blocks))
    x, planes = lax.optimization_barrier((x, planes))
    x = ordered(x)
    rank_out = swap_copied(after(rank_out, x))
    ranks = [[swap_copied(after(value[0], x)) for value in (rank_up, rank_down)]]
    partners = exchange([x] * 4)
    parts = low_rank_part(x, rows_in[0])
    gathered = [gather_columns(planes[0])]
    share = after(chip_sums(parts).astype(BF), gathered[0], partners[0], partners[2])
    latent = copied_all_to_all(share, 8, CUBE).reshape(HALF, RANK)
    latent = latent, pair(latent, "core")
    for layer in range(layers):
        last = layer == layers - 1
        weights = prep(orders[layer], gathered[layer])
        mine, other, own, *terms = mlp(x, partners, latent, weights, *ranks[layer])
        parts = core_sum(mine, other).astype(BF).reshape(8, HALF // 8, RANK)
        if not last:
            mine, other = share_of_core(dot(rank_out[layer], rows_in[layer + 1]))
            small = core_sum(mine, other).astype(BF).reshape(8, RANK // 16, RANK)
            parts = jnp.concatenate([parts, small], axis=1)
            gathered.append(gather_columns(after(planes[layer + 1], parts)))
            ranks.append(
                [swap_copied(after(value[layer + 1], own)) for value in (rank_up, rank_down)]
            )
        share = chip_sums(parts).astype(BF)
        terms = exchange(terms)
        t_zl, t_core, t_x0, t_x1 = terms
        t_core = jnp.concatenate([t_core[HALF:], t_core[:HALF]], axis=0)
        if last:
            share = after(share, terms[0], terms[3])
            back = copied_all_to_all(share, 8, CUBE).reshape(HALF, RANK)
            back = back, pair(back, "core")
        for term in (t_zl, t_core, t_x0, t_x1):
            own = own + term.astype(F32)
        if not last:
            parts = low_rank_part(own.astype(BF), rows_in[layer + 1])
            got = lax.all_to_all(
                jnp.concatenate(
                    [jnp.broadcast_to(share[None], (8,) + share.shape), parts], axis=1
                ),
                CUBE, 0, 0,
            )
            both = got[:, : HALF // 8 + RANK // 16]
            pair_both = pair(both, "core")
            back = both[:, : HALF // 8].reshape(HALF, RANK), pair_both[:, : HALF // 8].reshape(HALF, RANK)
            small = jnp.concatenate([both[:, HALF // 8 :], pair_both[:, HALF // 8 :]], axis=0)
            small = ordered(small.reshape(RANK, RANK))
            latent = jnp.sum(got[:, HALF // 8 + RANK // 16 :].astype(F32), axis=0)
            latent = latent + dot(share[: HALF // 8], small)
            latent = after(latent.astype(BF), gathered[layer + 1], *ranks[layer + 1])
            latent = copied_all_to_all(latent, 8, CUBE).reshape(HALF, RANK)
            latent = latent, pair(latent, "core")
        own = own + dot(jnp.concatenate(back, axis=0), rank_out[layer])
        x = own.astype(BF)
        if not last:
            partners = exchange([x] * 4)
    return swap(ordered(x))


def solution(mesh):
    fine = Mesh(mesh.devices.reshape((2,) * 8), TOK + FEAT)
    return jax.shard_map(
        per_device,
        mesh=fine,
        in_specs=(
            P(TOK, FEAT),
            P(),
            P(None, FEAT, None, None, TOK),
            P(None, FEAT, None, None, TOK),
            P(),
            P(None, None, FEAT),
            P(None, FEAT, None),
            P(None, None, FEAT),
        ),
        out_specs=P(TOK, FEAT),
        check_vma=False,
    )
```

```python
import functools

import jax
import jax.numpy as jnp
from jax import lax
from jax.experimental import pallas as pl
from jax.experimental.pallas import tpu as pltpu
from jax.sharding import Mesh, PartitionSpec as P

BF = jnp.bfloat16
F32 = jnp.float32
TOK = ("zl", "y1", "y0", "core")
FEAT = ("x1", "x0", "zh1", "zh0")
SWAPPED = ("zl", "core", "zh1", "zh0")
BIT_AXES = ("zl", "core", "x0", "x1")
CUBE = ("x1", "x0", "zl")


def pair(value, axis):
    return lax.ppermute(value, axis, [(0, 1), (1, 0)])


def bits(i):
    return i >> 3 & 1, i >> 2 & 1, i >> 1 & 1, i & 1


def index(zl, core, zh1, zh0):
    return zl << 3 | core << 2 | zh1 << 1 | zh0


def swap(value, k0=0, k1=0):
    perm = []
    for dst in range(16):
        zl, core, zh1, zh0 = bits(dst)
        perm.append((index(zh0 ^ k0, zh1 ^ k1, core, zl), dst))
    return lax.ppermute(value, SWAPPED, perm)


def swap_copied(value):
    perm = []
    for dst in range(16):
        zl, core, zh1, zh0 = bits(dst)
        perm.append((index(zh0 ^ zh1 ^ core, zh1, core, zl), dst))
    return lax.ppermute(value, SWAPPED, perm)


def copied_all_to_all(value, count, axes):
    return lax.all_to_all(jnp.broadcast_to(value[None], (count,) + value.shape), axes, 0, 0)


def after(value, *others):
    return lax.optimization_barrier((value,) + others)[0]


def nt_dot(left, right):
    return lax.dot_general(left, right, (((1,), (1,)), ((), ())), preferred_element_type=F32)


def dot(left, right):
    return jnp.dot(left, right, preferred_element_type=F32)


TILE = 256
TILES = 4
TOKENS = TILE * TILES
HALF = TOKENS // 2
WIDTH = 128
HIDDEN = 512
RANK = 256
CHUNK = HALF // 8
SMALL = RANK // 16
LIMIT = pltpu.CompilerParams(vmem_limit_bytes=56 << 20)


def ordered(rows):
    core = lax.axis_index("core")
    half = rows.shape[0] // 2
    return jnp.where(core == 0, rows, jnp.concatenate([rows[half:], rows[:half]], axis=0))


def prep_kernel(
    layer, bits, y, own, before, ahead, far0, far1, up_w, down_w, rank_up, rank_down
):
    whole = [
        (step, zl, ref, zl * 2) for step, ref in ((0, own), (3, before), (1, ahead)) for zl in range(2)
    ]
    pairs = whole + [(2, 0, far0, 0), (2, 1, far1, 0)]
    for step, zl, cols, first in pairs:
        chip = (y[0] + step) % 4
        for core in range(2):
            t = zl * 8 + chip * 2 + core
            piece = cols.at[first + core]
            for i in range(4):
                rank_up[pl.ds(pl.multiple_of(t * 16, 16), 16), i * 128 : (i + 1) * 128] = piece[
                    320 + i * 16 : 336 + i * 16, :
                ]
            for i in range(2):
                rank_down[pl.ds(pl.multiple_of(t * 32, 32), 32), i * 128 : (i + 1) * 128] = piece[
                    384 + i * 32 : 416 + i * 32, :
                ]
    for place in range(5):
        level = jnp.int32(0)
        if place > 0:
            for i in range(4):
                level = level + jnp.where(bits[layer, i] == place - 1, jnp.int32(1 + i), 0)
        at = pl.multiple_of(level * 32, 32)
        for step, zl, cols, first in pairs:
            chip = (y[0] + step) % 4
            pieces = []
            for core in range(2):
                t = zl * 8 + chip * 2 + core
                up_w[
                    pl.ds(pl.multiple_of(t * 32, 32), 32), place * WIDTH : (place + 1) * WIDTH
                ] = cols[first + core, pl.ds(at, 32), :]
                pieces.append(cols[first + core, pl.ds(160 + at, 32), :].astype(F32))
            top = pl.multiple_of(place * WIDTH + zl * 64 + chip * 16, 16)
            for q in range(4):
                down_w[pl.ds(top, 16), q * 128 : (q + 1) * 128] = jnp.concatenate(
                    [piece[q * 8 : (q + 1) * 8] for piece in pieces], axis=0
                ).astype(BF)


def prep(layer, level_bits, planes):
    y = lax.axis_index(("y1", "y0")).astype(jnp.int32).reshape(1)
    shapes = [(HIDDEN, 5 * WIDTH), (5 * WIDTH, HIDDEN), (RANK, HIDDEN), (HIDDEN, RANK)]
    return pl.pallas_call(
        functools.partial(prep_kernel, layer),
        grid_spec=pltpu.PrefetchScalarGridSpec(
            num_scalar_prefetch=2,
            grid=(1,),
            in_specs=[
                pl.BlockSpec(plane.shape, lambda i, *_: (0, 0, 0)) for plane in planes
            ],
            out_specs=[pl.BlockSpec(shape, lambda i, *_: (0, 0)) for shape in shapes],
        ),
        out_shape=[jax.ShapeDtypeStruct(shape, BF) for shape in shapes],
        compiler_params=LIMIT,
        cost_estimate=pl.CostEstimate(flops=2 << 30, bytes_accessed=6 << 20, transcendentals=0),
        name="prep",
    )(level_bits, y, *planes)


def gelu(value):
    return 0.5 * value * (1.0 + lax.erf(value * (0.5**0.5)))


def mlp_kernel(
    x, p_zl, p_core, p_x0, p_x1, mine, other, up_w, down_w, rank_up, rank_down, *rest
):
    small, (mine_back, other_back, own, t_zl, t_core, t_x0, t_x1) = rest[:-7], rest[-7:]
    i = pl.program_id(0)
    value = x[...]
    left = jnp.concatenate([value, p_zl[...], p_core[...], p_x0[...], p_x1[...]], axis=1)
    latent = jnp.where(i < 2, mine[...], other[...])
    pre = nt_dot(left, up_w[...]) + dot(latent, rank_up[...])
    hidden = gelu(pre).astype(BF)
    share = dot(hidden, rank_down[...]).astype(BF).reshape(TILE // CHUNK, CHUNK, RANK)
    for half, back in enumerate((mine_back, other_back)):

        @pl.when(i // 2 == half)
        def _():
            back[:, :CHUNK] = share
            if small:
                back[:, CHUNK:] = small[half][...]

    terms = nt_dot(hidden, down_w[...])
    own[...] = value.astype(F32) + terms[:, :WIDTH]
    for bit, out in enumerate((t_zl, t_core, t_x0, t_x1)):
        out[...] = terms[:, (1 + bit) * WIDTH : (2 + bit) * WIDTH].astype(BF)


def mlp(x, partners, latent, weights, small):
    row = pl.BlockSpec((TILE, WIDTH), lambda i: (i, 0))
    partner_row = pl.BlockSpec((TILE, WIDTH), lambda i: ((i + 2) % TILES, 0))
    halves = lambda n: [
        pl.BlockSpec((TILE // CHUNK, n, RANK), lambda i: (jnp.minimum(i, 1), 0, 0)),
        pl.BlockSpec((TILE // CHUNK, n, RANK), lambda i: (jnp.maximum(i - 2, 0), 0, 0)),
    ]
    latents = [
        pl.BlockSpec((TILE, RANK), lambda i: (jnp.minimum(i, 1), 0)),
        pl.BlockSpec((TILE, RANK), lambda i: (jnp.maximum(i - 2, 0), 0)),
    ]
    whole = lambda *shape: pl.BlockSpec(shape, lambda i: (0,) * len(shape))
    shape = jax.ShapeDtypeStruct
    rows = CHUNK + (SMALL if small else 0)
    return pl.pallas_call(
        mlp_kernel,
        grid=(TILES,),
        in_specs=[row, row, partner_row, row, row]
        + latents
        + [
            whole(HIDDEN, 5 * WIDTH),
            whole(5 * WIDTH, HIDDEN),
            whole(RANK, HIDDEN),
            whole(HIDDEN, RANK),
        ]
        + (halves(SMALL) if small else []),
        out_specs=halves(rows) + [row] * 5,
        out_shape=[shape((8, rows, RANK), BF)] * 2
        + [shape((TOKENS, WIDTH), F32)]
        + [shape((TOKENS, WIDTH), BF)] * 4,
        compiler_params=LIMIT,
        cost_estimate=pl.CostEstimate(
            flops=4 * TOKENS * HIDDEN * (5 * WIDTH + RANK),
            bytes_accessed=6 << 20,
            transcendentals=0,
        ),
        name="mlp",
    )(x, *partners, *latent, *weights, *small)


def split_kernel(got, back, small, latent):
    back[...] = got[:, :CHUNK]
    small[...] = got[:, CHUNK : CHUNK + SMALL]
    total = got[0, CHUNK + SMALL :].astype(F32)
    for i in range(1, 8):
        total = total + got[i, CHUNK + SMALL :].astype(F32)
    latent[...] = total


def split(got):
    shapes = [(8, CHUNK, RANK), (8, SMALL, RANK), (CHUNK, RANK)]
    whole = lambda shape: pl.BlockSpec(shape, lambda i: (0,) * len(shape))
    return pl.pallas_call(
        split_kernel,
        grid=(1,),
        in_specs=[whole(got.shape)],
        out_specs=[whole(shape) for shape in shapes],
        out_shape=[jax.ShapeDtypeStruct(s, t) for s, t in zip(shapes, (BF, BF, F32))],
        compiler_params=LIMIT,
        cost_estimate=pl.CostEstimate(flops=1 << 20, bytes_accessed=1 << 20, transcendentals=0),
        name="split",
    )(got)


def chip_sums(parts):
    return jnp.sum(lax.all_to_all(parts, CUBE, 0, 0).astype(F32), axis=0)


def core_sum(mine, other):
    return mine.astype(F32) + pair(other.astype(BF), "core").astype(F32)


def share_of_core(rows):
    core = lax.axis_index("core")
    half = rows.shape[0] // 2
    return (
        lax.dynamic_slice_in_dim(rows, core * half, half, 0),
        lax.dynamic_slice_in_dim(rows, (1 - core) * half, half, 0),
    )


def pack_kernel(t, cols, up_rows, down_rows, out):
    del t
    out[:, :320] = cols[...]
    for i in range(4):
        out[:, 320 + i * 16 : 336 + i * 16] = up_rows[:, :, i * 128 : (i + 1) * 128]
    for i in range(2):
        out[:, 384 + i * 32 : 416 + i * 32] = down_rows[:, :, i * 128 : (i + 1) * 128]


def block_shards(up_blocks, down_blocks, rank_up, rank_down):
    layers = up_blocks.shape[0]
    t = lax.axis_index(TOK)
    up_shard = up_blocks[:, 0].transpose(0, 1, 3, 2).reshape(layers, 160, 128)
    down_shard = down_blocks[:, 0].reshape(layers, 5, 4, 128, 8).transpose(0, 1, 2, 4, 3)
    cols = jnp.concatenate([up_shard, down_shard.reshape(layers, 160, 128)], axis=1)
    shape = (layers, 448, 128)
    return pl.pallas_call(
        pack_kernel,
        grid_spec=pltpu.PrefetchScalarGridSpec(
            num_scalar_prefetch=1,
            grid=(1,),
            in_specs=[
                pl.BlockSpec(cols.shape, lambda i, t: (0, 0, 0)),
                pl.BlockSpec((layers, 16, HIDDEN), lambda i, t: (0, t[0], 0)),
                pl.BlockSpec((layers, 32, RANK), lambda i, t: (0, t[0], 0)),
            ],
            out_specs=pl.BlockSpec(shape, lambda i, t: (0, 0, 0)),
        ),
        out_shape=jax.ShapeDtypeStruct(shape, BF),
        compiler_params=LIMIT,
        cost_estimate=pl.CostEstimate(flops=1 << 20, bytes_accessed=1 << 19, transcendentals=0),
        name="pack",
    )(t.astype(jnp.int32).reshape(1), cols, rank_up, rank_down)


def gather_planes(shards):
    zh0, zh1 = lax.axis_index("zh0"), lax.axis_index("zh1")
    outs = [jnp.zeros((4,) + shards.shape[1:], shards.dtype)] * shards.shape[0]
    for k0 in range(2):
        for k1 in range(2):
            got = swap(shards, k0, k1)
            at = (zh0 ^ k0) * 2 + (zh1 ^ k1)
            outs = [
                lax.dynamic_update_slice(out, got[i : i + 1], (at, 0, 0))
                for i, out in enumerate(outs)
            ]
    return outs


def along_y(value, step):
    return lax.ppermute(value, ("y1", "y0"), [(i, (i + step) % 4) for i in range(4)])


def near_columns(plane):
    return [plane, along_y(plane, 1), along_y(plane, -1)]


def far_columns(before, ahead):
    return [along_y(before[:2], 1), along_y(ahead[2:], -1)]


def low_rank_part(x, rows_in):
    other = dot(x[HALF:], rows_in)
    return core_sum(dot(x[:HALF], rows_in), other).astype(BF).reshape(8, HALF // 8, RANK)


def exchange(blocks):
    return [pair(value, axis) for value, axis in zip(blocks, BIT_AXES)]


def per_device(tokens, level_bits, up_blocks, down_blocks, rank_in, rank_up, rank_down, rank_out):
    layers = level_bits.shape[0]
    core = lax.axis_index("core")
    block = lax.axis_index("x1") * 8 + lax.axis_index("x0") * 4 + core * 2 + lax.axis_index("zl")
    rows_in = lax.dynamic_slice(rank_in, (0, block * WIDTH, 0), (layers, WIDTH, RANK))
    planes = gather_planes(block_shards(up_blocks, down_blocks, rank_up, rank_down))
    x = ordered(swap(tokens))
    partners = exchange([x] * 4)
    parts, rank_out, *planes = lax.optimization_barrier(
        (low_rank_part(x, rows_in[0]), swap_copied(rank_out), *planes)
    )
    near = near_columns(planes[0])
    share = chip_sums(parts).astype(BF)
    share = after(share, *near, partners[0], partners[2])
    gathered = [near + far_columns(*near[1:])]
    latent = copied_all_to_all(share, 8, CUBE).reshape(HALF, RANK)
    for layer in range(layers):
        last = layer == layers - 1
        cols = lax.optimization_barrier((x, *gathered[layer]))[1:]
        weights = prep(layer, level_bits, cols)
        if layer == 0:
            latent = after(latent, *weights)
        small = []
        if not last:
            small = share_of_core(dot(rank_out[layer], rows_in[layer + 1]).astype(BF))
            small = [part.reshape(8, SMALL, RANK) for part in small]
        mine, other, own, *terms = mlp(
            x, partners, (latent, pair(latent, "core")), weights, small
        )
        parts = core_sum(mine, other).astype(BF)
        terms = exchange(terms)
        if not last:
            near = near_columns(after(planes[layer + 1], latent))
        share = chip_sums(parts).astype(BF)
        if not last:
            share, own = lax.optimization_barrier((share, own))
            share = after(share, *near)
            gathered.append(near + far_columns(*near[1:]))
        t_zl, t_core, t_x0, t_x1 = terms
        t_core = jnp.concatenate([t_core[HALF:], t_core[:HALF]], axis=0)
        if last:
            share = after(share, terms[0], terms[3])
            back = copied_all_to_all(share, 8, CUBE)
        for term in (t_zl, t_core, t_x0, t_x1):
            own = own + term.astype(F32)
        if not last:
            parts = low_rank_part(own.astype(BF), rows_in[layer + 1])
            got = lax.all_to_all(
                jnp.concatenate(
                    [jnp.broadcast_to(share[None], (8,) + share.shape), parts], axis=1
                ),
                CUBE, 0, 0,
            )
            back, small, latent = split(after(got, *gathered[layer + 1]))
            small = small.reshape(RANK // 2, RANK)
            small = ordered(jnp.concatenate([small, pair(small, "core")], axis=0))
            back = back.reshape(HALF, RANK)
            back = jnp.concatenate([back, pair(back, "core")], axis=0)
            x = (own + dot(back, rank_out[layer])).astype(BF)
            partners = exchange([x] * 4)
            latent = after(latent, x)
            latent = (latent + dot(share[:CHUNK], small)).astype(BF)
            latent = copied_all_to_all(latent, 8, CUBE).reshape(HALF, RANK)
    back = back.reshape(HALF, RANK)
    back = jnp.concatenate([back, pair(back, "core")], axis=0)
    x = (own + dot(back, rank_out[layers - 1])).astype(BF)
    return swap(ordered(x))


def solution(mesh):
    fine = Mesh(mesh.devices.reshape((2,) * 8), TOK + FEAT)
    return jax.shard_map(
        per_device,
        mesh=fine,
        in_specs=(
            P(TOK, FEAT),
            P(),
            P(None, FEAT, None, None, TOK),
            P(None, FEAT, None, None, TOK),
            P(),
            P(None, None, FEAT),
            P(None, FEAT, None),
            P(None, None, FEAT),
        ),
        out_specs=P(TOK, FEAT),
        check_vma=False,
    )
```

```python
import functools

import jax
import jax.numpy as jnp
from jax import lax
from jax.experimental import pallas as pl
from jax.experimental.pallas import tpu as pltpu
from jax.sharding import Mesh, PartitionSpec as P

BF = jnp.bfloat16
F32 = jnp.float32
TOK = ("zl", "y1", "y0", "core")
FEAT = ("x1", "x0", "zh1", "zh0")
SWAPPED = ("zl", "core", "zh1", "zh0")
BIT_AXES = ("zl", "core", "x0", "x1")
CUBE = ("x1", "x0", "zl")


def pair(value, axis):
    return lax.ppermute(value, axis, [(0, 1), (1, 0)])


def bits(i):
    return i >> 3 & 1, i >> 2 & 1, i >> 1 & 1, i & 1


def index(zl, core, zh1, zh0):
    return zl << 3 | core << 2 | zh1 << 1 | zh0


def swap(value, k0=0, k1=0):
    perm = []
    for dst in range(16):
        zl, core, zh1, zh0 = bits(dst)
        perm.append((index(zh0 ^ k0, zh1 ^ k1, core, zl), dst))
    return lax.ppermute(value, SWAPPED, perm)


def swap_copied(value):
    perm = []
    for dst in range(16):
        zl, core, zh1, zh0 = bits(dst)
        perm.append((index(zh0 ^ zh1 ^ core, zh1, core, zl), dst))
    return lax.ppermute(value, SWAPPED, perm)


def copied_all_to_all(value, count, axes):
    return lax.all_to_all(jnp.broadcast_to(value[None], (count,) + value.shape), axes, 0, 0)


def after(value, *others):
    return lax.optimization_barrier((value,) + others)[0]


def nt_dot(left, right):
    return lax.dot_general(left, right, (((1,), (1,)), ((), ())), preferred_element_type=F32)


def dot(left, right):
    return jnp.dot(left, right, preferred_element_type=F32)


TILE = 512
TILES = 2
TOKENS = TILE * TILES
HALF = TOKENS // 2
WIDTH = 128
HIDDEN = 512
RANK = 256
CHUNK = HALF // 8
SMALL = RANK // 16
LIMIT = pltpu.CompilerParams(vmem_limit_bytes=56 << 20)


def ordered(rows):
    core = lax.axis_index("core")
    half = rows.shape[0] // 2
    return jnp.where(core == 0, rows, jnp.concatenate([rows[half:], rows[:half]], axis=0))


def prep_kernel(
    layer, bits, y, own, before, ahead, far0, far1, up_w, down_w, rank_up, rank_down
):
    whole = [
        (step, zl, ref, zl * 2) for step, ref in ((0, own), (3, before), (1, ahead)) for zl in range(2)
    ]
    pairs = whole + [(2, 0, far0, 0), (2, 1, far1, 0)]
    for step, zl, cols, first in pairs:
        chip = (y[0] + step) % 4
        for core in range(2):
            t = zl * 8 + chip * 2 + core
            piece = cols.at[first + core]
            for i in range(4):
                rank_up[pl.ds(pl.multiple_of(t * 16, 16), 16), i * 128 : (i + 1) * 128] = piece[
                    320 + i * 16 : 336 + i * 16, :
                ]
            for i in range(2):
                rank_down[pl.ds(pl.multiple_of(t * 32, 32), 32), i * 128 : (i + 1) * 128] = piece[
                    384 + i * 32 : 416 + i * 32, :
                ]
    for place in range(5):
        level = jnp.int32(0)
        if place > 0:
            for i in range(4):
                level = level + jnp.where(bits[layer, i] == place - 1, jnp.int32(1 + i), 0)
        at = pl.multiple_of(level * 32, 32)
        for step, zl, cols, first in pairs:
            chip = (y[0] + step) % 4
            pieces = []
            for core in range(2):
                t = zl * 8 + chip * 2 + core
                up_w[
                    pl.ds(pl.multiple_of(t * 32, 32), 32), place * WIDTH : (place + 1) * WIDTH
                ] = cols[first + core, pl.ds(at, 32), :]
                pieces.append(cols[first + core, pl.ds(160 + at, 32), :].astype(F32))
            top = pl.multiple_of(place * WIDTH + zl * 64 + chip * 16, 16)
            for q in range(4):
                down_w[pl.ds(top, 16), q * 128 : (q + 1) * 128] = jnp.concatenate(
                    [piece[q * 8 : (q + 1) * 8] for piece in pieces], axis=0
                ).astype(BF)


def prep(layer, level_bits, planes):
    y = lax.axis_index(("y1", "y0")).astype(jnp.int32).reshape(1)
    shapes = [(HIDDEN, 5 * WIDTH), (5 * WIDTH, HIDDEN), (RANK, HIDDEN), (HIDDEN, RANK)]
    return pl.pallas_call(
        functools.partial(prep_kernel, layer),
        grid_spec=pltpu.PrefetchScalarGridSpec(
            num_scalar_prefetch=2,
            grid=(1,),
            in_specs=[
                pl.BlockSpec(plane.shape, lambda i, *_: (0, 0, 0)) for plane in planes
            ],
            out_specs=[pl.BlockSpec(shape, lambda i, *_: (0, 0)) for shape in shapes],
        ),
        out_shape=[jax.ShapeDtypeStruct(shape, BF) for shape in shapes],
        compiler_params=LIMIT,
        cost_estimate=pl.CostEstimate(flops=2 << 30, bytes_accessed=6 << 20, transcendentals=0),
        name="prep",
    )(level_bits, y, *planes)


def gelu(value):
    return 0.5 * value * (1.0 + lax.erf(value * (0.5**0.5)))


def mlp_kernel(
    x, p_zl, p_core, p_x0, p_x1, mine, other, up_w, down_w, rank_up, rank_down, *rest
):
    small, (mine_back, other_back, own, t_zl, t_core, t_x0, t_x1) = rest[:-7], rest[-7:]
    i = pl.program_id(0)
    value = x[...]
    left = jnp.concatenate([value, p_zl[...], p_core[...], p_x0[...], p_x1[...]], axis=1)
    latent = jnp.where(i < TILES // 2, mine[...], other[...])
    pre = nt_dot(left, up_w[...]) + dot(latent, rank_up[...])
    hidden = gelu(pre).astype(BF)
    share = dot(hidden, rank_down[...]).astype(BF).reshape(TILE // CHUNK, CHUNK, RANK)
    for half, back in enumerate((mine_back, other_back)):

        @pl.when(i // (TILES // 2) == half)
        def _():
            back[:, :CHUNK] = share
            if small:
                back[:, CHUNK:] = small[half][...]

    terms = nt_dot(hidden, down_w[...])
    own[...] = value.astype(F32) + terms[:, :WIDTH]
    for bit, out in enumerate((t_zl, t_core, t_x0, t_x1)):
        out[...] = terms[:, (1 + bit) * WIDTH : (2 + bit) * WIDTH].astype(BF)


def mlp(x, partners, latent, weights, small):
    row = pl.BlockSpec((TILE, WIDTH), lambda i: (i, 0))
    partner_row = pl.BlockSpec((TILE, WIDTH), lambda i: ((i + TILES // 2) % TILES, 0))
    halves = lambda n: [
        pl.BlockSpec((TILE // CHUNK, n, RANK), lambda i: (jnp.minimum(i, TILES // 2 - 1), 0, 0)),
        pl.BlockSpec((TILE // CHUNK, n, RANK), lambda i: (jnp.maximum(i - TILES // 2, 0), 0, 0)),
    ]
    latents = [
        pl.BlockSpec((TILE, RANK), lambda i: (jnp.minimum(i, TILES // 2 - 1), 0)),
        pl.BlockSpec((TILE, RANK), lambda i: (jnp.maximum(i - TILES // 2, 0), 0)),
    ]
    whole = lambda *shape: pl.BlockSpec(shape, lambda i: (0,) * len(shape))
    shape = jax.ShapeDtypeStruct
    rows = CHUNK + (SMALL if small else 0)
    return pl.pallas_call(
        mlp_kernel,
        grid=(TILES,),
        in_specs=[row, row, partner_row, row, row]
        + latents
        + [
            whole(HIDDEN, 5 * WIDTH),
            whole(5 * WIDTH, HIDDEN),
            whole(RANK, HIDDEN),
            whole(HIDDEN, RANK),
        ]
        + (halves(SMALL) if small else []),
        out_specs=halves(rows) + [row] * 5,
        out_shape=[shape((8, rows, RANK), BF)] * 2
        + [shape((TOKENS, WIDTH), F32)]
        + [shape((TOKENS, WIDTH), BF)] * 4,
        compiler_params=LIMIT,
        cost_estimate=pl.CostEstimate(
            flops=4 * TOKENS * HIDDEN * (5 * WIDTH + RANK),
            bytes_accessed=6 << 20,
            transcendentals=0,
        ),
        name="mlp",
    )(x, *partners, *latent, *weights, *small)


def split_kernel(got, back, small, latent):
    back[...] = got[:, :CHUNK]
    small[...] = got[:, CHUNK : CHUNK + SMALL]
    total = got[0, CHUNK + SMALL :].astype(F32)
    for i in range(1, 8):
        total = total + got[i, CHUNK + SMALL :].astype(F32)
    latent[...] = total


def split(got):
    shapes = [(8, CHUNK, RANK), (8, SMALL, RANK), (CHUNK, RANK)]
    whole = lambda shape: pl.BlockSpec(shape, lambda i: (0,) * len(shape))
    return pl.pallas_call(
        split_kernel,
        grid=(1,),
        in_specs=[whole(got.shape)],
        out_specs=[whole(shape) for shape in shapes],
        out_shape=[jax.ShapeDtypeStruct(s, t) for s, t in zip(shapes, (BF, BF, F32))],
        compiler_params=LIMIT,
        cost_estimate=pl.CostEstimate(flops=1 << 20, bytes_accessed=1 << 20, transcendentals=0),
        name="split",
    )(got)


def chip_sums(parts):
    return jnp.sum(lax.all_to_all(parts, CUBE, 0, 0).astype(F32), axis=0)


def core_sum(mine, other):
    return mine.astype(F32) + pair(other.astype(BF), "core").astype(F32)


def share_of_core(rows):
    core = lax.axis_index("core")
    half = rows.shape[0] // 2
    return (
        lax.dynamic_slice_in_dim(rows, core * half, half, 0),
        lax.dynamic_slice_in_dim(rows, (1 - core) * half, half, 0),
    )


def pack_kernel(t, cols, up_rows, down_rows, out):
    del t
    out[:, :320] = cols[...]
    for i in range(4):
        out[:, 320 + i * 16 : 336 + i * 16] = up_rows[:, :, i * 128 : (i + 1) * 128]
    for i in range(2):
        out[:, 384 + i * 32 : 416 + i * 32] = down_rows[:, :, i * 128 : (i + 1) * 128]


def block_shards(up_blocks, down_blocks, rank_up, rank_down):
    layers = up_blocks.shape[0]
    t = lax.axis_index(TOK)
    up_shard = up_blocks[:, 0].transpose(0, 1, 3, 2).reshape(layers, 160, 128)
    down_shard = down_blocks[:, 0].reshape(layers, 5, 4, 128, 8).transpose(0, 1, 2, 4, 3)
    cols = jnp.concatenate([up_shard, down_shard.reshape(layers, 160, 128)], axis=1)
    shape = (layers, 448, 128)
    return pl.pallas_call(
        pack_kernel,
        grid_spec=pltpu.PrefetchScalarGridSpec(
            num_scalar_prefetch=1,
            grid=(1,),
            in_specs=[
                pl.BlockSpec(cols.shape, lambda i, t: (0, 0, 0)),
                pl.BlockSpec((layers, 16, HIDDEN), lambda i, t: (0, t[0], 0)),
                pl.BlockSpec((layers, 32, RANK), lambda i, t: (0, t[0], 0)),
            ],
            out_specs=pl.BlockSpec(shape, lambda i, t: (0, 0, 0)),
        ),
        out_shape=jax.ShapeDtypeStruct(shape, BF),
        compiler_params=LIMIT,
        cost_estimate=pl.CostEstimate(flops=1 << 20, bytes_accessed=1 << 19, transcendentals=0),
        name="pack",
    )(t.astype(jnp.int32).reshape(1), cols, rank_up, rank_down)


def gather_planes(shards):
    zh0, zh1 = lax.axis_index("zh0"), lax.axis_index("zh1")
    outs = [jnp.zeros((4,) + shards.shape[1:], shards.dtype)] * shards.shape[0]
    for k0 in range(2):
        for k1 in range(2):
            got = swap(shards, k0, k1)
            at = (zh0 ^ k0) * 2 + (zh1 ^ k1)
            outs = [
                lax.dynamic_update_slice(out, got[i : i + 1], (at, 0, 0))
                for i, out in enumerate(outs)
            ]
    return outs


def along_y(value, step):
    return lax.ppermute(value, ("y1", "y0"), [(i, (i + step) % 4) for i in range(4)])


def near_columns(plane):
    return [plane, along_y(plane, 1), along_y(plane, -1)]


def far_columns(before, ahead):
    return [along_y(before[:2], 1), along_y(ahead[2:], -1)]


def low_rank_part(x, rows_in):
    other = dot(x[HALF:], rows_in)
    return core_sum(dot(x[:HALF], rows_in), other).astype(BF).reshape(8, HALF // 8, RANK)


def exchange(blocks):
    return [pair(value, axis) for value, axis in zip(blocks, BIT_AXES)]


def per_device(tokens, level_bits, up_blocks, down_blocks, rank_in, rank_up, rank_down, rank_out):
    layers = level_bits.shape[0]
    core = lax.axis_index("core")
    block = lax.axis_index("x1") * 8 + lax.axis_index("x0") * 4 + core * 2 + lax.axis_index("zl")
    rows_in = lax.dynamic_slice(rank_in, (0, block * WIDTH, 0), (layers, WIDTH, RANK))
    planes = gather_planes(block_shards(up_blocks, down_blocks, rank_up, rank_down))
    x = ordered(swap(tokens))
    partners = exchange([x] * 4)
    parts, rank_out, *planes = lax.optimization_barrier(
        (low_rank_part(x, rows_in[0]), swap_copied(rank_out), *planes)
    )
    near = near_columns(planes[0])
    share = chip_sums(parts).astype(BF)
    share = after(share, *near, partners[0], partners[2])
    gathered = [near + far_columns(*near[1:])]
    latent = copied_all_to_all(share, 8, CUBE).reshape(HALF, RANK)
    for layer in range(layers):
        last = layer == layers - 1
        cols = lax.optimization_barrier((x, *gathered[layer]))[1:]
        weights = prep(layer, level_bits, cols)
        if layer == 0:
            latent = after(latent, *weights)
        small = []
        if not last:
            small = share_of_core(dot(rank_out[layer], rows_in[layer + 1]).astype(BF))
            small = [part.reshape(8, SMALL, RANK) for part in small]
        mine, other, own, *terms = mlp(
            x, partners, (latent, pair(latent, "core")), weights, small
        )
        parts = core_sum(mine, other).astype(BF)
        terms = exchange(terms)
        if not last:
            near = near_columns(after(planes[layer + 1], latent))
        share = chip_sums(parts).astype(BF)
        if not last:
            own = after(own, parts, *near)
            share = after(share, *near)
            gathered.append(near + far_columns(*near[1:]))
        t_zl, t_core, t_x0, t_x1 = terms
        t_core = jnp.concatenate([t_core[HALF:], t_core[:HALF]], axis=0)
        if last:
            share = after(share, terms[0], terms[3])
            back = copied_all_to_all(share, 8, CUBE)
        for term in (t_zl, t_core, t_x0, t_x1):
            own = own + term.astype(F32)
        if not last:
            parts = low_rank_part(own.astype(BF), rows_in[layer + 1])
            got = lax.all_to_all(
                jnp.concatenate(
                    [jnp.broadcast_to(share[None], (8,) + share.shape), parts], axis=1
                ),
                CUBE, 0, 0,
            )
            back, small, latent = split(after(got, *gathered[layer + 1]))
            small = small.reshape(RANK // 2, RANK)
            small = ordered(jnp.concatenate([small, pair(small, "core")], axis=0))
            back = back.reshape(HALF, RANK)
            back = jnp.concatenate([back, pair(back, "core")], axis=0)
            x = (own + dot(back, rank_out[layer])).astype(BF)
            partners = exchange([x] * 4)
            latent = after(latent, x)
            latent = (latent + dot(share[:CHUNK], small)).astype(BF)
            latent = copied_all_to_all(latent, 8, CUBE).reshape(HALF, RANK)
    back = back.reshape(HALF, RANK)
    back = jnp.concatenate([back, pair(back, "core")], axis=0)
    x = (own + dot(back, rank_out[layers - 1])).astype(BF)
    return swap(ordered(x))


def solution(mesh):
    fine = Mesh(mesh.devices.reshape((2,) * 8), TOK + FEAT)
    return jax.shard_map(
        per_device,
        mesh=fine,
        in_specs=(
            P(TOK, FEAT),
            P(),
            P(None, FEAT, None, None, TOK),
            P(None, FEAT, None, None, TOK),
            P(),
            P(None, None, FEAT),
            P(None, FEAT, None),
            P(None, None, FEAT),
        ),
        out_specs=P(TOK, FEAT),
        check_vma=False,
    )
```

```python
import functools

import jax
import jax.numpy as jnp
from jax import lax
from jax.experimental import pallas as pl
from jax.experimental.pallas import tpu as pltpu
from jax.sharding import Mesh, PartitionSpec as P

BF = jnp.bfloat16
F32 = jnp.float32
TOK = ("zl", "y1", "y0", "core")
FEAT = ("x1", "x0", "zh1", "zh0")
SWAPPED = ("zl", "core", "zh1", "zh0")
BIT_AXES = ("zl", "core", "x0", "x1")
CUBE = ("x1", "x0", "zl")


def pair(value, axis):
    return lax.ppermute(value, axis, [(0, 1), (1, 0)])


def bits(i):
    return i >> 3 & 1, i >> 2 & 1, i >> 1 & 1, i & 1


def index(zl, core, zh1, zh0):
    return zl << 3 | core << 2 | zh1 << 1 | zh0


def swap(value, k0=0, k1=0):
    perm = []
    for dst in range(16):
        zl, core, zh1, zh0 = bits(dst)
        perm.append((index(zh0 ^ k0, zh1 ^ k1, core, zl), dst))
    return lax.ppermute(value, SWAPPED, perm)


def swap_copied(value):
    perm = []
    for dst in range(16):
        zl, core, zh1, zh0 = bits(dst)
        perm.append((index(zh0 ^ zh1 ^ core, zh1, core, zl), dst))
    return lax.ppermute(value, SWAPPED, perm)


def copied_all_to_all(value, count, axes):
    return lax.all_to_all(jnp.broadcast_to(value[None], (count,) + value.shape), axes, 0, 0)


def after(value, *others):
    return lax.optimization_barrier((value,) + others)[0]


def nt_dot(left, right):
    return lax.dot_general(left, right, (((1,), (1,)), ((), ())), preferred_element_type=F32)


def dot(left, right):
    return jnp.dot(left, right, preferred_element_type=F32)


TILE = 512
TILES = 2
TOKENS = TILE * TILES
HALF = TOKENS // 2
WIDTH = 128
HIDDEN = 512
RANK = 256
CHUNK = HALF // 8
SMALL = RANK // 16
LIMIT = pltpu.CompilerParams(vmem_limit_bytes=56 << 20)


def ordered(rows):
    core = lax.axis_index("core")
    half = rows.shape[0] // 2
    return jnp.where(core == 0, rows, jnp.concatenate([rows[half:], rows[:half]], axis=0))


def prep_kernel(
    layer, bits, y, own, before, ahead, far0, far1, up_w, down_w, rank_up, rank_down
):
    whole = [
        (step, zl, ref, zl * 2) for step, ref in ((0, own), (3, before), (1, ahead)) for zl in range(2)
    ]
    pairs = whole + [(2, 0, far0, 0), (2, 1, far1, 0)]
    for step, zl, cols, first in pairs:
        chip = (y[0] + step) % 4
        for core in range(2):
            t = zl * 8 + chip * 2 + core
            piece = cols.at[first + core]
            for i in range(4):
                rank_up[pl.ds(pl.multiple_of(t * 16, 16), 16), i * 128 : (i + 1) * 128] = piece[
                    320 + i * 16 : 336 + i * 16, :
                ]
            for i in range(2):
                rank_down[pl.ds(pl.multiple_of(t * 32, 32), 32), i * 128 : (i + 1) * 128] = piece[
                    384 + i * 32 : 416 + i * 32, :
                ]
    for place in range(5):
        level = jnp.int32(0)
        if place > 0:
            for i in range(4):
                level = level + jnp.where(bits[layer, i] == place - 1, jnp.int32(1 + i), 0)
        at = pl.multiple_of(level * 32, 32)
        for step, zl, cols, first in pairs:
            chip = (y[0] + step) % 4
            pieces = []
            for core in range(2):
                t = zl * 8 + chip * 2 + core
                up_w[
                    pl.ds(pl.multiple_of(t * 32, 32), 32), place * WIDTH : (place + 1) * WIDTH
                ] = cols[first + core, pl.ds(at, 32), :]
                pieces.append(cols[first + core, pl.ds(160 + at, 32), :].astype(F32))
            top = pl.multiple_of(place * WIDTH + zl * 64 + chip * 16, 16)
            for q in range(4):
                down_w[pl.ds(top, 16), q * 128 : (q + 1) * 128] = jnp.concatenate(
                    [piece[q * 8 : (q + 1) * 8] for piece in pieces], axis=0
                ).astype(BF)


def prep(layer, level_bits, planes):
    y = lax.axis_index(("y1", "y0")).astype(jnp.int32).reshape(1)
    shapes = [(HIDDEN, 5 * WIDTH), (5 * WIDTH, HIDDEN), (RANK, HIDDEN), (HIDDEN, RANK)]
    return pl.pallas_call(
        functools.partial(prep_kernel, layer),
        grid_spec=pltpu.PrefetchScalarGridSpec(
            num_scalar_prefetch=2,
            grid=(1,),
            in_specs=[
                pl.BlockSpec(plane.shape, lambda i, *_: (0, 0, 0)) for plane in planes
            ],
            out_specs=[pl.BlockSpec(shape, lambda i, *_: (0, 0)) for shape in shapes],
        ),
        out_shape=[jax.ShapeDtypeStruct(shape, BF) for shape in shapes],
        compiler_params=LIMIT,
        cost_estimate=pl.CostEstimate(flops=2 << 30, bytes_accessed=6 << 20, transcendentals=0),
        name="prep",
    )(level_bits, y, *planes)


def gelu(value):
    return 0.5 * value * (1.0 + lax.erf(value * (0.5**0.5)))


def mlp_kernel(
    x, p_zl, p_core, p_x0, p_x1, mine, other, up_w, down_w, rank_up, rank_down, *rest
):
    small, (mine_back, other_back, own, t_zl, t_core, t_x0, t_x1) = rest[:-7], rest[-7:]
    i = pl.program_id(0)
    value = x[...]
    left = jnp.concatenate([value, p_zl[...], p_core[...], p_x0[...], p_x1[...]], axis=1)
    latent = jnp.where(i < TILES // 2, mine[...], other[...])
    pre = nt_dot(left, up_w[...]) + dot(latent, rank_up[...])
    hidden = gelu(pre).astype(BF)
    share = dot(hidden, rank_down[...]).astype(BF).reshape(TILE // CHUNK, CHUNK, RANK)
    for half, back in enumerate((mine_back, other_back)):

        @pl.when(i // (TILES // 2) == half)
        def _():
            back[:, :CHUNK] = share
            if small:
                back[:, CHUNK:] = small[half][...]

    terms = nt_dot(hidden, down_w[...])
    own[...] = value.astype(F32) + terms[:, :WIDTH]
    for bit, out in enumerate((t_zl, t_core, t_x0, t_x1)):
        out[...] = terms[:, (1 + bit) * WIDTH : (2 + bit) * WIDTH].astype(BF)


def mlp(x, partners, latent, weights, small):
    row = pl.BlockSpec((TILE, WIDTH), lambda i: (i, 0))
    partner_row = pl.BlockSpec((TILE, WIDTH), lambda i: ((i + TILES // 2) % TILES, 0))
    halves = lambda n: [
        pl.BlockSpec((TILE // CHUNK, n, RANK), lambda i: (jnp.minimum(i, TILES // 2 - 1), 0, 0)),
        pl.BlockSpec((TILE // CHUNK, n, RANK), lambda i: (jnp.maximum(i - TILES // 2, 0), 0, 0)),
    ]
    latents = [
        pl.BlockSpec((TILE, RANK), lambda i: (jnp.minimum(i, TILES // 2 - 1), 0)),
        pl.BlockSpec((TILE, RANK), lambda i: (jnp.maximum(i - TILES // 2, 0), 0)),
    ]
    whole = lambda *shape: pl.BlockSpec(shape, lambda i: (0,) * len(shape))
    shape = jax.ShapeDtypeStruct
    rows = CHUNK + (SMALL if small else 0)
    return pl.pallas_call(
        mlp_kernel,
        grid=(TILES,),
        in_specs=[row, row, partner_row, row, row]
        + latents
        + [
            whole(HIDDEN, 5 * WIDTH),
            whole(5 * WIDTH, HIDDEN),
            whole(RANK, HIDDEN),
            whole(HIDDEN, RANK),
        ]
        + (halves(SMALL) if small else []),
        out_specs=halves(rows) + [row] * 5,
        out_shape=[shape((8, rows, RANK), BF)] * 2
        + [shape((TOKENS, WIDTH), F32)]
        + [shape((TOKENS, WIDTH), BF)] * 4,
        compiler_params=LIMIT,
        cost_estimate=pl.CostEstimate(
            flops=4 * TOKENS * HIDDEN * (5 * WIDTH + RANK),
            bytes_accessed=6 << 20,
            transcendentals=0,
        ),
        name="mlp",
    )(x, *partners, *latent, *weights, *small)


def split_kernel(got, back, small, latent):
    back[...] = got[:, :CHUNK]
    small[...] = got[:, CHUNK : CHUNK + SMALL]
    total = got[0, CHUNK + SMALL :].astype(F32)
    for i in range(1, 8):
        total = total + got[i, CHUNK + SMALL :].astype(F32)
    latent[...] = total


def split(got):
    shapes = [(8, CHUNK, RANK), (8, SMALL, RANK), (CHUNK, RANK)]
    whole = lambda shape: pl.BlockSpec(shape, lambda i: (0,) * len(shape))
    return pl.pallas_call(
        split_kernel,
        grid=(1,),
        in_specs=[whole(got.shape)],
        out_specs=[whole(shape) for shape in shapes],
        out_shape=[jax.ShapeDtypeStruct(s, t) for s, t in zip(shapes, (BF, BF, F32))],
        compiler_params=LIMIT,
        cost_estimate=pl.CostEstimate(flops=1 << 20, bytes_accessed=1 << 20, transcendentals=0),
        name="split",
    )(got)


def chip_sums(parts):
    return jnp.sum(lax.all_to_all(parts, CUBE, 0, 0).astype(F32), axis=0)


def core_sum(mine, other):
    return mine.astype(F32) + pair(other.astype(BF), "core").astype(F32)


def share_of_core(rows):
    core = lax.axis_index("core")
    half = rows.shape[0] // 2
    return (
        lax.dynamic_slice_in_dim(rows, core * half, half, 0),
        lax.dynamic_slice_in_dim(rows, (1 - core) * half, half, 0),
    )


def pack_kernel(t, cols, up_rows, down_rows, out):
    del t
    out[:, :320] = cols[...]
    for i in range(4):
        out[:, 320 + i * 16 : 336 + i * 16] = up_rows[:, :, i * 128 : (i + 1) * 128]
    for i in range(2):
        out[:, 384 + i * 32 : 416 + i * 32] = down_rows[:, :, i * 128 : (i + 1) * 128]


def block_shards(up_blocks, down_blocks, rank_up, rank_down):
    layers = up_blocks.shape[0]
    t = lax.axis_index(TOK)
    up_shard = up_blocks[:, 0].transpose(0, 1, 3, 2).reshape(layers, 160, 128)
    down_shard = down_blocks[:, 0].reshape(layers, 5, 4, 128, 8).transpose(0, 1, 2, 4, 3)
    cols = jnp.concatenate([up_shard, down_shard.reshape(layers, 160, 128)], axis=1)
    shape = (layers, 448, 128)
    return pl.pallas_call(
        pack_kernel,
        grid_spec=pltpu.PrefetchScalarGridSpec(
            num_scalar_prefetch=1,
            grid=(1,),
            in_specs=[
                pl.BlockSpec(cols.shape, lambda i, t: (0, 0, 0)),
                pl.BlockSpec((layers, 16, HIDDEN), lambda i, t: (0, t[0], 0)),
                pl.BlockSpec((layers, 32, RANK), lambda i, t: (0, t[0], 0)),
            ],
            out_specs=pl.BlockSpec(shape, lambda i, t: (0, 0, 0)),
        ),
        out_shape=jax.ShapeDtypeStruct(shape, BF),
        compiler_params=LIMIT,
        cost_estimate=pl.CostEstimate(flops=1 << 20, bytes_accessed=1 << 19, transcendentals=0),
        name="pack",
    )(t.astype(jnp.int32).reshape(1), cols, rank_up, rank_down)


def gather_planes(shards):
    zh0, zh1 = lax.axis_index("zh0"), lax.axis_index("zh1")
    outs = [jnp.zeros((4,) + shards.shape[1:], shards.dtype)] * shards.shape[0]
    for k0 in range(2):
        for k1 in range(2):
            got = swap(shards, k0, k1)
            at = (zh0 ^ k0) * 2 + (zh1 ^ k1)
            outs = [
                lax.dynamic_update_slice(out, got[i : i + 1], (at, 0, 0))
                for i, out in enumerate(outs)
            ]
    return outs


def along_y(value, step):
    return lax.ppermute(value, ("y1", "y0"), [(i, (i + step) % 4) for i in range(4)])


def near_columns(plane):
    return [plane, along_y(plane, 1), along_y(plane, -1)]


def far_columns(before, ahead):
    return [along_y(before[:2], 1), along_y(ahead[2:], -1)]


def low_rank_part(x, rows_in):
    other = dot(x[HALF:], rows_in)
    return core_sum(dot(x[:HALF], rows_in), other).astype(BF).reshape(8, HALF // 8, RANK)


def exchange(blocks):
    return [pair(value, axis) for value, axis in zip(blocks, BIT_AXES)]


def per_device(tokens, level_bits, up_blocks, down_blocks, rank_in, rank_up, rank_down, rank_out):
    layers = level_bits.shape[0]
    core = lax.axis_index("core")
    block = lax.axis_index("x1") * 8 + lax.axis_index("x0") * 4 + core * 2 + lax.axis_index("zl")
    rows_in = lax.dynamic_slice(rank_in, (0, block * WIDTH, 0), (layers, WIDTH, RANK))
    planes = gather_planes(block_shards(up_blocks, down_blocks, rank_up, rank_down))
    x = ordered(swap(tokens))
    partners = exchange([x] * 4)
    parts, rank_out, *planes = lax.optimization_barrier(
        (low_rank_part(x, rows_in[0]), swap_copied(rank_out), *planes)
    )
    near = near_columns(planes[0])
    share = chip_sums(parts).astype(BF)
    smalls = [
        [
            part.reshape(8, SMALL, RANK)
            for part in share_of_core(dot(rank_out[i], rows_in[i + 1]).astype(BF))
        ]
        for i in range(layers - 1)
    ]
    share = after(share, *near, partners[0], partners[2], *sum(smalls, []))
    gathered = [near + far_columns(*near[1:])]
    latent = copied_all_to_all(share, 8, CUBE).reshape(HALF, RANK)
    for layer in range(layers):
        last = layer == layers - 1
        cols = lax.optimization_barrier((x, *gathered[layer]))[1:]
        weights = prep(layer, level_bits, cols)
        if layer == 0:
            latent = after(latent, *weights)
        small = [] if last else smalls[layer]
        mine, other, own, *terms = mlp(
            x, partners, (latent, pair(latent, "core")), weights, small
        )
        parts = core_sum(mine, other).astype(BF)
        terms = exchange(terms)
        if not last:
            near = near_columns(after(planes[layer + 1], latent))
        share = chip_sums(parts).astype(BF)
        if not last:
            own = after(own, parts, *near)
            share = after(share, *near)
            gathered.append(near + far_columns(*near[1:]))
        t_zl, t_core, t_x0, t_x1 = terms
        t_core = jnp.concatenate([t_core[HALF:], t_core[:HALF]], axis=0)
        if last:
            share = after(share, terms[0], terms[3])
            back = copied_all_to_all(share, 8, CUBE)
        for term in (t_zl, t_core, t_x0, t_x1):
            own = own + term.astype(F32)
        if not last:
            parts = low_rank_part(own.astype(BF), rows_in[layer + 1])
            got = lax.all_to_all(
                jnp.concatenate(
                    [jnp.broadcast_to(share[None], (8,) + share.shape), parts], axis=1
                ),
                CUBE, 0, 0,
            )
            back, small, latent = split(after(got, *gathered[layer + 1]))
            small = small.reshape(RANK // 2, RANK)
            small = ordered(jnp.concatenate([small, pair(small, "core")], axis=0))
            back = back.reshape(HALF, RANK)
            back = jnp.concatenate([back, pair(back, "core")], axis=0)
            x = (own + dot(back, rank_out[layer])).astype(BF)
            partners = exchange([x] * 4)
            latent = after(latent, x)
            latent = (latent + dot(share[:CHUNK], small)).astype(BF)
            latent = copied_all_to_all(latent, 8, CUBE).reshape(HALF, RANK)
    back = back.reshape(HALF, RANK)
    back = jnp.concatenate([back, pair(back, "core")], axis=0)
    x = (own + dot(back, rank_out[layers - 1])).astype(BF)
    return swap(ordered(x))


def solution(mesh):
    fine = Mesh(mesh.devices.reshape((2,) * 8), TOK + FEAT)
    return jax.shard_map(
        per_device,
        mesh=fine,
        in_specs=(
            P(TOK, FEAT),
            P(),
            P(None, FEAT, None, None, TOK),
            P(None, FEAT, None, None, TOK),
            P(),
            P(None, None, FEAT),
            P(None, FEAT, None),
            P(None, None, FEAT),
        ),
        out_specs=P(TOK, FEAT),
        check_vma=False,
    )
```
